768 devices in a mesh: blk: 192 (over z, x, y_lo, core), group: 4 (over y_hi).
Axes of the slice: x: 4, y: 8 (y_hi: 4, y_lo: 2; y = y_hi * 2 + y_lo), z: 12, core: 2. Of those that a mesh axis runs over, the one named last changes fastest.
Arguments:
- audio_embed: bfloat16 [196608, 768], P(('blk', 'group')), may hold values from -0.19921875 to 0.19921875
- text_embed: bfloat16 [196608, 768], P(('blk', 'group')), may hold values from -0.19921875 to 0.19921875
- caption_ids: int32 [196608], P(('blk', 'group')), may hold values from 0 to 4095
- pairing: int32 [4], replicated, may hold values from 0 to 3, each once
- logit_scale: float32 [1], replicated, may hold values from 3 to 15
- logit_bias: float32 [1], replicated, may hold values from -4 to 0
Outputs:
- loss: float32 [], replicated
- grad_audio: bfloat16 [196608, 768], P(('blk', 'group'))
- grad_text: bfloat16 [196608, 768], P(('blk', 'group'))
The draws below stay inside these ranges and needn't reach their ends.
Inputs may be any that keep to these rules, and one draw needn't show every extreme that they name: `pairing`: a permutation of the group indices.
All inputs are finite; a program needn't handle non-finite values.
Results may differ from the reference program's by a relative error of at most 0.0011.
The reference program's roundings to bfloat16 on the way (of `coeff`) count: a program that leaves them out, or rounds other values in their place, can miss the bound.
Values may be sent and summed in bfloat16 or wider, within the bound.
No kernel may reach another device: no remote copies, remote signals or barrier semaphores. Data moves between devices by JAX's collectives and lax.ppermute only.
A program may use at most 32 MiB of HBM per device.

```python
import math
import jax
import jax.numpy as jnp
import numpy as np
from jax import lax

D = 768
ROWS = 256
ROUNDS = 4
PAIRS = 196608
N_BLK = 192
N_GROUP = 4


def with_ends(result, stream_key, least, top_value):
    longest = result.shape.index(max(result.shape))
    spots = []
    for shift in (0, 1):
        where = [jax.random.randint(jax.random.fold_in(stream_key, axis), (), 0, length) for axis, length in enumerate(result.shape)]
        where[longest] = (where[longest] + shift) % result.shape[longest]
        spots.append(tuple(where))
    return result.at[spots[0]].set(least).at[spots[1]].set(top_value)


def levels(rng, extent, pieces, least, high):
    def one(position, shards_of):
        steps = jax.random.uniform(jax.random.fold_in(jax.random.fold_in(rng, 6), position), (shards_of,), jnp.float32, least / len(pieces), high / len(pieces))
        return jnp.repeat(jnp.exp(steps), extent[position] // shards_of).reshape((-1,) + (1,) * (len(extent) - position - 1))

    level = one(*pieces[0])
    for cut in pieces[1:]:
        level = level * one(*cut)
    return level


def cumulative_ranks(count, lean):
    portions = [(1 << 20) // math.isqrt(grade ** lean) + 1 for grade in range(1, count + 1)]
    deviation = 1 + sum(portions) // (1 << 30)
    return np.cumsum(np.array([max(1, weight // deviation) for weight in portions]))


def skewed_ids(rng, extent, amount, slope):
    table = cumulative_ranks(amount, slope)
    lot = jax.random.randint(jax.random.fold_in(rng, 1), extent, 0, int(table[amount - 1]))
    rank = jnp.searchsorted(jnp.asarray(table, jnp.int32), lot, side="right")
    return jax.random.permutation(jax.random.fold_in(rng, 2), amount)[rank].astype(jnp.int32)


def centred(rng, dims, width, most, cuts=(), held_as=jnp.bfloat16):
    factor_of = levels(rng, dims, cuts, -0.22, 0.18) if cuts else 1.0
    values = jax.random.normal(rng, dims, jnp.float32) * width * factor_of
    return jnp.minimum(jnp.maximum(values, -most), most).astype(held_as)


def setup_inputs(seed: int = 0) -> dict:
    key_list = jax.random.split(jax.random.key(seed), 7)
    audio_embed = centred(key_list[0], (PAIRS, D), 0.036, 0.19921875, ((0, 768),))
    text_embed = centred(key_list[1], (PAIRS, D), 0.036, 0.19921875, ((0, 768),))
    caption_ids = with_ends(skewed_ids(key_list[2], (PAIRS,), 4096, 2), jax.random.fold_in(key_list[2], 3), 0, 4095).astype(jnp.int32)
    pairing = jax.random.permutation(key_list[3], N_GROUP).astype(jnp.int32)
    logit_scale = jnp.clip(jnp.exp(jax.random.uniform(key_list[4], (1,), jnp.float32, math.log(3.0), math.log(15.0))), 3.0, 15.0)
    logit_bias = jnp.clip(jax.random.uniform(key_list[5], (1,), jnp.float32, -4.0, 0.0), -4.0, 0.0)
    return dict(audio_embed=audio_embed, text_embed=text_embed, caption_ids=caption_ids, pairing=pairing, logit_scale=logit_scale, logit_bias=logit_bias)


def pair_terms(audio, audio_ids, text, text_ids, scale, bias):
    dots = jnp.einsum("brd,bsd->brs", audio.astype(jnp.float32), text.astype(jnp.float32))
    logits = scale * dots + bias
    sign = jnp.where(audio_ids[:, :, None] == text_ids[:, None, :], 1.0, -1.0).astype(jnp.float32)
    margin = sign * logits
    total = jnp.sum(jax.nn.softplus(-margin))
    coeff = (-scale * sign * jax.nn.sigmoid(-margin)).astype(jnp.bfloat16)
    coeff = lax.optimization_barrier(coeff).astype(jnp.float32)
    grad_a = jnp.einsum("brs,bsd->brd", coeff, text.astype(jnp.float32))
    grad_t = jnp.einsum("brs,brd->bsd", coeff, audio.astype(jnp.float32))
    return total, grad_a, grad_t


def reference(audio_embed, text_embed, caption_ids, pairing, logit_scale, logit_bias):
    blocks = N_BLK * N_GROUP
    audio = audio_embed.reshape(N_BLK, N_GROUP, ROWS, D)
    text = text_embed.reshape(N_BLK, N_GROUP, ROWS, D)
    ids = caption_ids.reshape(N_BLK, N_GROUP, ROWS)
    scale = logit_scale[0]
    bias = logit_bias[0]
    flat_audio = audio.reshape(blocks, ROWS, D)
    flat_ids = ids.reshape(blocks, ROWS)

    def run(text_blocks, text_ids):
        total, grad_a, grad_t = pair_terms(flat_audio, flat_ids, text_blocks.reshape(blocks, ROWS, D), text_ids.reshape(blocks, ROWS), scale, bias)
        return total, grad_a.reshape(N_BLK, N_GROUP, ROWS, D), grad_t.reshape(N_BLK, N_GROUP, ROWS, D)

    loss_total, grad_audio, grad_text = run(text, ids)
    for shift in range(1, ROUNDS + 1):
        total, grad_a, grad_t = run(jnp.roll(text, shift, axis=0), jnp.roll(ids, shift, axis=0))
        loss_total = loss_total + total
        grad_audio = grad_audio + grad_a
        grad_text = grad_text + jnp.roll(grad_t, -shift, axis=0)
    total, grad_a, grad_t = run(text[:, pairing], ids[:, pairing])
    loss_total = loss_total + total
    grad_audio = grad_audio + grad_a
    grad_text = grad_text.at[:, pairing].add(grad_t)
    loss = loss_total / jnp.float32(PAIRS)
    return loss, grad_audio.reshape(PAIRS, D).astype(jnp.bfloat16), grad_text.reshape(PAIRS, D).astype(jnp.bfloat16)
```

```python
import functools
import itertools

import jax
import jax.numpy as jnp
import numpy as np
from jax import lax
from jax.experimental import pallas as pl
from jax.experimental.pallas import tpu as pltpu
from jax.sharding import PartitionSpec as P

SPLIT = 64
MARKS = 16
AXES = ("z", "x", "yl", "core", "group")
BLK = AXES[:4]
PERMS = list(itertools.permutations(range(4)))


def shifted(array, by):
    count = lax.axis_size(BLK)
    return lax.ppermute(array, BLK, [(i, (i + by) % count) for i in range(count)])


def core_swap(array):
    return lax.ppermute(array, "core", [(0, 1), (1, 0)])


def after(array, *earlier):
    return lax.optimization_barrier((array,) + earlier)[0]


def pair_margin(scale, bias, ids, mine, other):
    rows = ids.shape[0]
    dots = lax.dot_general(
        mine, other[:rows, :], (((1,), (1,)), ((), ())), preferred_element_type=jnp.float32
    )
    marks = other[rows:, :rows].astype(jnp.float32)
    same = ids == marks[0:1] * SPLIT + marks[1:2]
    logits = scale * dots + bias
    return same, jnp.where(same, logits, -logits)


def start_loads(sources, targets, sems):
    for i, (source, target) in enumerate(zip(sources, targets)):
        pltpu.make_async_copy(source, target, sems.at[i]).start()


def wait_load(source, target, sems, i):
    pltpu.make_async_copy(source, target, sems.at[i]).wait()


def loss_kernel(n_text, count, scalars, own_ids, audio, text, *refs):
    others = refs[:count]
    out, own, held, sems = refs[count:]
    start_loads(
        (audio, text) + others, [own.at[0], own.at[1]] + [held.at[i] for i in range(count)], sems
    )
    wait_load(audio, own.at[0], sems, 0)
    wait_load(text, own.at[1], sems, 1)
    rows = own_ids.shape[0]
    total = jnp.zeros((1, rows), jnp.float32)
    for i in range(-1, count):
        kind = 1 if i >= n_text else 0
        other = own.at[1] if i < 0 else held.at[i]
        if i >= 0:
            wait_load(text, held.at[i], sems, i + 2)
        _, margin = pair_margin(scalars[0], scalars[1], own_ids[...], own[kind, :rows, :], other)
        tail = jnp.log1p(jnp.exp(-jnp.abs(margin)))
        total += jnp.sum(jnp.maximum(-margin, 0.0) + tail, axis=0, keepdims=True)
    out[...] = total[:, :128] + total[:, 128:]


def grad_kernel(n_text, count, scalars, own_ids, audio, text, *refs):
    others = refs[:count]
    grad_audio, grad_text, own, held, sems = refs[count:]
    rows = own_ids.shape[0]
    start_loads(
        (audio, text) + others, [own.at[0], own.at[1]] + [held.at[i] for i in range(count)], sems
    )
    wait_load(audio, own.at[0], sems, 0)
    wait_load(text, own.at[1], sems, 1)

    def term(mine, other):
        scale = scalars[0]
        same, margin = pair_margin(scale, scalars[1], own_ids[...], mine[:rows, :], other)
        tail = jnp.exp(-jnp.abs(margin))
        weight = jnp.where(margin >= 0.0, tail, 1.0) / (1.0 + tail)
        coeff = (jnp.where(same, -scale, scale) * weight).astype(jnp.bfloat16)
        return jnp.dot(coeff, other[:rows, :], preferred_element_type=jnp.float32)

    for kind, (grad, indices) in enumerate(
        ((grad_audio, range(n_text)), (grad_text, range(n_text, count)))
    ):
        acc = term(own.at[kind], own.at[1 - kind])
        for i in indices:
            wait_load(text, held.at[i], sems, i + 2)
            acc += term(own.at[kind], held.at[i])
        grad[...] = acc.astype(jnp.bfloat16)


def call(kernel, scalars, own_ids, audio, text, texts, audios, out_shape, flops):
    blocks = tuple(texts) + tuple(audios)
    count = len(blocks)
    whole = pl.BlockSpec(memory_space=pltpu.VMEM)
    anywhere = pl.BlockSpec(memory_space=pl.ANY)
    return pl.pallas_call(
        functools.partial(kernel, len(texts), count),
        out_shape=out_shape,
        in_specs=[pl.BlockSpec(memory_space=pltpu.SMEM), whole] + [anywhere] * (2 + count),
        out_specs=jax.tree.map(lambda _: whole, out_shape),
        scratch_shapes=[
            pltpu.VMEM((2,) + text.shape, text.dtype),
            pltpu.VMEM((count,) + text.shape, text.dtype),
            pltpu.SemaphoreType.DMA((2 + count,)),
        ],
        compiler_params=pltpu.CompilerParams(vmem_limit_bytes=24 * 1024 * 1024),
        cost_estimate=pl.CostEstimate(
            flops=flops, bytes_accessed=2 * (count + 2) * text.size, transcendentals=0
        ),
    )(scalars, own_ids, audio, text, *blocks)


def losses(scalars, own_ids, audio, text, texts, audios):
    rows = own_ids.shape[0]
    return call(
        loss_kernel,
        scalars,
        own_ids,
        audio,
        text,
        texts,
        audios,
        jax.ShapeDtypeStruct((1, 128), jnp.float32),
        2 * (1 + len(texts) + len(audios)) * rows * text.size,
    )


def gradients(scalars, own_ids, audio, text, texts, audios):
    rows = own_ids.shape[0]
    shape = (rows, text.shape[1])
    return call(
        grad_kernel,
        scalars,
        own_ids,
        audio,
        text,
        texts,
        audios,
        [jax.ShapeDtypeStruct(shape, jnp.bfloat16)] * 2,
        4 * (2 + len(texts) + len(audios)) * rows * text.size,
    )


def spread_sum(row, axes):
    count = lax.axis_size(axes)
    copies = jnp.broadcast_to(row[None], (count,) + row.shape)
    return jnp.sum(lax.all_to_all(copies, axes, 0, 0, tiled=True), axis=0)


def exchange(perm, text, audio):
    first = lax.axis_index("core") == 0
    forward = [(p, g) for g, p in enumerate(perm)]
    backward = [(g, p) for g, p in enumerate(perm)]
    partner_text, partner_audio = text, audio
    moved = forward != [(g, g) for g in range(len(perm))]
    text4 = shifted(text, 4)
    audio2 = shifted(audio, -2)
    if moved:
        partner_text = lax.ppermute(text, "group", forward)
    text2 = shifted(text, 2)
    audio4 = shifted(audio, -4)
    if moved:
        source = after(audio, partner_text) if set(forward) == set(backward) else audio
        partner_audio = lax.ppermute(source, "group", backward)
    text_x = core_swap(jnp.where(first, text, text4))
    audio_x = core_swap(audio2)
    text_y = core_swap(text2)
    audio_y = core_swap(jnp.where(first, audio4, audio))
    return (
        (text4, text_x, partner_text, text2, text_y),
        (audio2, audio_x, audio4, audio_y, partner_audio),
    )


def body(audio_embed, text_embed, caption_ids, pairing, logit_scale, logit_bias):
    rows, width = audio_embed.shape
    pair_count = rows * lax.axis_size(AXES)
    scalars = jnp.concatenate([logit_scale, logit_bias])
    high = (caption_ids // SPLIT).astype(jnp.bfloat16)
    low = (caption_ids % SPLIT).astype(jnp.bfloat16)
    marks = jnp.pad(jnp.stack([high, low]), ((0, MARKS - 2), (0, width - rows)))
    text = jnp.concatenate([text_embed, marks])
    audio = jnp.concatenate([audio_embed, marks])
    own_ids = caption_ids.astype(jnp.float32).reshape(rows, 1)
    index = jnp.argmax(jnp.all(jnp.asarray(np.array(PERMS, np.int32)) == pairing[None], axis=1))
    texts, audios = lax.switch(
        index, [functools.partial(exchange, perm) for perm in PERMS], text, audio
    )
    terms = losses(scalars, own_ids, audio, text, texts[:3], audios[:2])
    total = spread_sum(spread_sum(terms, ("yl", "core", "group")), ("z", "x"))
    grad_audio, grad_text = gradients(scalars, own_ids, audio, text, texts, audios)
    return jnp.sum(total) / jnp.float32(pair_count), grad_audio, grad_text


def solution(mesh):
    inner = jax.sharding.Mesh(mesh.devices.reshape(12, 4, 2, 2, 4), AXES)
    placed = (P(AXES, None), P(AXES, None), P(AXES), P(), P(), P())
    return jax.shard_map(
        body,
        mesh=inner,
        in_specs=placed,
        out_specs=(P(), P(AXES, None), P(AXES, None)),
        check_vma=False,
    )
```

```python
import functools
import itertools

import jax
import jax.numpy as jnp
import numpy as np
from jax import lax
from jax.experimental import pallas as pl
from jax.experimental.pallas import tpu as pltpu
from jax.sharding import PartitionSpec as P

SPLIT = 64
MARKS = 16
AXES = ("z", "x", "yl", "core", "group")
BLK = AXES[:4]
PERMS = list(itertools.permutations(range(4)))


def shifted(array, by):
    count = lax.axis_size(BLK)
    return lax.ppermute(array, BLK, [(i, (i + by) % count) for i in range(count)])


def core_swap(array):
    return lax.ppermute(array, "core", [(0, 1), (1, 0)])


def after(array, *earlier):
    return lax.optimization_barrier((array,) + earlier)[0]


def pair_margin(scale, bias, ids, mine, other):
    rows = ids.shape[0]
    dots = lax.dot_general(
        mine, other[:rows, :], (((1,), (1,)), ((), ())), preferred_element_type=jnp.float32
    )
    marks = other[rows:, :rows].astype(jnp.float32)
    same = ids == marks[0:1] * SPLIT + marks[1:2]
    logits = scale * dots + bias
    return same, jnp.where(same, logits, -logits)


def start_loads(sources, targets, sems):
    for i, (source, target) in enumerate(zip(sources, targets)):
        pltpu.make_async_copy(source, target, sems.at[i]).start()


def wait_load(source, target, sems, i):
    pltpu.make_async_copy(source, target, sems.at[i]).wait()


def loss_kernel(n_text, count, scalars, own_ids, audio, text, *refs):
    others = refs[:count]
    out, own, held, sems = refs[count:]
    start_loads(
        (audio, text) + others, [own.at[0], own.at[1]] + [held.at[i] for i in range(count)], sems
    )
    wait_load(audio, own.at[0], sems, 0)
    wait_load(text, own.at[1], sems, 1)
    rows = own_ids.shape[0]
    total = jnp.zeros((1, rows), jnp.float32)
    for i in range(-1, count):
        kind = 1 if i >= n_text else 0
        other = own.at[1] if i < 0 else held.at[i]
        if i >= 0:
            wait_load(text, held.at[i], sems, i + 2)
        _, margin = pair_margin(scalars[0], scalars[1], own_ids[...], own[kind, :rows, :], other)
        total += jnp.sum(jnp.maximum(-margin, 0.0), axis=0, keepdims=True)
        tail = jnp.exp(-jnp.abs(margin))
        while tail.shape[0] > 8:
            half = tail.shape[0] // 2
            upper, lower = tail[:half], tail[half:]
            tail = upper + lower + upper * lower
        total += jnp.sum(jnp.log1p(tail), axis=0, keepdims=True)
    out[...] = total[:, :128] + total[:, 128:]


def grad_kernel(n_text, count, scalars, own_ids, audio, text, *refs):
    others = refs[:count]
    grad_audio, grad_text, own, held, sems = refs[count:]
    rows = own_ids.shape[0]
    start_loads(
        (audio, text) + others, [own.at[0], own.at[1]] + [held.at[i] for i in range(count)], sems
    )
    wait_load(audio, own.at[0], sems, 0)
    wait_load(text, own.at[1], sems, 1)

    def term(mine, other):
        scale = scalars[0]
        same, margin = pair_margin(scale, scalars[1], own_ids[...], mine[:rows, :], other)
        tail = jnp.exp(-jnp.abs(margin))
        weight = jnp.where(margin >= 0.0, tail, 1.0) / (1.0 + tail)
        coeff = (jnp.where(same, -scale, scale) * weight).astype(jnp.bfloat16)
        return jnp.dot(coeff, other[:rows, :], preferred_element_type=jnp.float32)

    for kind, (grad, indices) in enumerate(
        ((grad_audio, range(n_text)), (grad_text, range(n_text, count)))
    ):
        acc = term(own.at[kind], own.at[1 - kind])
        for i in indices:
            wait_load(text, held.at[i], sems, i + 2)
            acc += term(own.at[kind], held.at[i])
        grad[...] = acc.astype(jnp.bfloat16)


def call(kernel, scalars, own_ids, audio, text, texts, audios, out_shape, flops):
    blocks = tuple(texts) + tuple(audios)
    count = len(blocks)
    whole = pl.BlockSpec(memory_space=pltpu.VMEM)
    anywhere = pl.BlockSpec(memory_space=pl.ANY)
    return pl.pallas_call(
        functools.partial(kernel, len(texts), count),
        out_shape=out_shape,
        in_specs=[pl.BlockSpec(memory_space=pltpu.SMEM), whole] + [anywhere] * (2 + count),
        out_specs=jax.tree.map(lambda _: whole, out_shape),
        scratch_shapes=[
            pltpu.VMEM((2,) + text.shape, text.dtype),
            pltpu.VMEM((count,) + text.shape, text.dtype),
            pltpu.SemaphoreType.DMA((2 + count,)),
        ],
        compiler_params=pltpu.CompilerParams(vmem_limit_bytes=24 * 1024 * 1024),
        cost_estimate=pl.CostEstimate(
            flops=flops, bytes_accessed=2 * (count + 2) * text.size, transcendentals=0
        ),
    )(scalars, own_ids, audio, text, *blocks)


def losses(scalars, own_ids, audio, text, texts, audios):
    rows = own_ids.shape[0]
    return call(
        loss_kernel,
        scalars,
        own_ids,
        audio,
        text,
        texts,
        audios,
        jax.ShapeDtypeStruct((1, 128), jnp.float32),
        2 * (1 + len(texts) + len(audios)) * rows * text.size,
    )


def gradients(scalars, own_ids, audio, text, texts, audios):
    rows = own_ids.shape[0]
    shape = (rows, text.shape[1])
    return call(
        grad_kernel,
        scalars,
        own_ids,
        audio,
        text,
        texts,
        audios,
        [jax.ShapeDtypeStruct(shape, jnp.bfloat16)] * 2,
        4 * (2 + len(texts) + len(audios)) * rows * text.size,
    )


def spread_sum(row, axes):
    count = lax.axis_size(axes)
    copies = jnp.broadcast_to(row[None], (count,) + row.shape)
    return jnp.sum(lax.all_to_all(copies, axes, 0, 0, tiled=True), axis=0)


def routed(array, step):
    count = lax.axis_size(BLK)
    return lax.ppermute(array, BLK, [(i, (i + step(i)) % count) for i in range(count)])


def odd(i):
    return i % 2 == 1


def group_pairs(perm):
    forward = [(p, g) for g, p in enumerate(perm)]
    backward = [(g, p) for g, p in enumerate(perm)]
    return forward, backward, all(p == g for g, p in enumerate(perm))


def first_exchange(perm, text, audio):
    forward, _, same = group_pairs(perm)
    partner_text = text if same else lax.ppermute(text, "group", forward)
    audio2 = shifted(audio, -2)
    text4 = shifted(text, 4)
    text_x = routed(text, lambda i: 3 if odd(i) else 1)
    audio_x = core_swap(audio2)
    return (text4, text_x, partner_text), (audio2, audio_x)


def second_exchange(perm, text, audio, terms):
    _, backward, same = group_pairs(perm)
    partner_audio = audio if same else lax.ppermute(audio, "group", backward)
    text2 = shifted(text, 2)
    audio4 = shifted(audio, -4)
    audio_y = routed(audio, lambda i: -1 if odd(i) else -3)
    row = spread_sum(terms, ("z",))
    return row, (audio_y, audio4), (partner_audio, text2)


def body(audio_embed, text_embed, caption_ids, pairing, logit_scale, logit_bias):
    rows, width = audio_embed.shape
    pair_count = rows * lax.axis_size(AXES)
    scalars = jnp.concatenate([logit_scale, logit_bias])
    high = (caption_ids // SPLIT).astype(jnp.bfloat16)
    low = (caption_ids % SPLIT).astype(jnp.bfloat16)
    marks = jnp.pad(jnp.stack([high, low]), ((0, MARKS - 2), (0, width - rows)))
    text = jnp.concatenate([text_embed, marks])
    audio = jnp.concatenate([audio_embed, marks])
    own_ids = caption_ids.astype(jnp.float32).reshape(rows, 1)
    index = jnp.argmax(jnp.all(jnp.asarray(np.array(PERMS, np.int32)) == pairing[None], axis=1))
    texts, audios = lax.switch(
        index, [functools.partial(first_exchange, perm) for perm in PERMS], text, audio
    )
    terms = losses(scalars, own_ids, audio, text, texts, audios)
    row, (audio_y, audio4), (partner_audio, text2) = lax.switch(
        index, [functools.partial(second_exchange, perm) for perm in PERMS], text, audio, terms
    )
    text_y = core_swap(text2)
    total = spread_sum(after(row, text_y), ("x", "yl", "core", "group"))
    grad_audio, grad_text = gradients(
        scalars,
        own_ids,
        audio,
        text,
        texts + (text2, text_y),
        audios + (audio4, audio_y, partner_audio),
    )
    return jnp.sum(total) / jnp.float32(pair_count), grad_audio, grad_text


def solution(mesh):
    inner = jax.sharding.Mesh(mesh.devices.reshape(12, 4, 2, 2, 4), AXES)
    placed = (P(AXES, None), P(AXES, None), P(AXES), P(), P(), P())
    return jax.shard_map(
        body,
        mesh=inner,
        in_specs=placed,
        out_specs=(P(), P(AXES, None), P(AXES, None)),
        check_vma=False,
    )
```

```python
import functools
import itertools

import jax
import jax.numpy as jnp
import numpy as np
from jax import lax
from jax.experimental import pallas as pl
from jax.experimental.pallas import tpu as pltpu
from jax.sharding import PartitionSpec as P

SPLIT = 64
MARKS = 16
AXES = ("z", "x", "yl", "core", "group")
BLK = AXES[:4]
PERMS = list(itertools.permutations(range(4)))


def shifted(array, by):
    count = lax.axis_size(BLK)
    return lax.ppermute(array, BLK, [(i, (i + by) % count) for i in range(count)])


def core_swap(array):
    return lax.ppermute(array, "core", [(0, 1), (1, 0)])


def after(array, *earlier):
    return lax.optimization_barrier((array,) + earlier)[0]


def pair_margin(scale, bias, ids, mine, other):
    rows = ids.shape[0]
    dots = lax.dot_general(
        mine, other[:rows, :], (((1,), (1,)), ((), ())), preferred_element_type=jnp.float32
    )
    marks = other[rows:, :rows].astype(jnp.float32)
    same = ids == marks[0:1] * SPLIT + marks[1:2]
    logits = scale * dots + bias
    return same, jnp.where(same, logits, -logits)


def start_loads(sources, targets, sems):
    for i, (source, target) in enumerate(zip(sources, targets)):
        pltpu.make_async_copy(source, target, sems.at[i]).start()


def wait_load(source, target, sems, i):
    pltpu.make_async_copy(source, target, sems.at[i]).wait()


def loss_kernel(n_text, count, scalars, own_ids, audio, text, *refs):
    others = refs[:count]
    out, own, held, sems = refs[count:]
    start_loads(
        (audio, text) + others, [own.at[0], own.at[1]] + [held.at[i] for i in range(count)], sems
    )
    wait_load(audio, own.at[0], sems, 0)
    wait_load(text, own.at[1], sems, 1)
    rows = own_ids.shape[0]
    total = jnp.zeros((1, rows), jnp.float32)
    for i in range(-1, count):
        kind = 1 if i >= n_text else 0
        other = own.at[1] if i < 0 else held.at[i]
        if i >= 0:
            wait_load(text, held.at[i], sems, i + 2)
        _, margin = pair_margin(scalars[0], scalars[1], own_ids[...], own[kind, :rows, :], other)
        total += jnp.sum(jnp.maximum(-margin, 0.0), axis=0, keepdims=True)
        tail = jnp.exp(-jnp.abs(margin))
        while tail.shape[0] > 8:
            half = tail.shape[0] // 2
            upper, lower = tail[:half], tail[half:]
            tail = upper + lower + upper * lower
        total += jnp.sum(jnp.log1p(tail), axis=0, keepdims=True)
    out[...] = total[:, :128] + total[:, 128:]


def grad_kernel(n_text, count, scalars, own_ids, audio, text, *refs):
    others = refs[:count]
    grad_audio, grad_text, own, held, sems = refs[count:]
    rows = own_ids.shape[0]
    start_loads(
        (audio, text) + others, [own.at[0], own.at[1]] + [held.at[i] for i in range(count)], sems
    )
    wait_load(audio, own.at[0], sems, 0)
    wait_load(text, own.at[1], sems, 1)

    def term(mine, other):
        scale = scalars[0]
        same, margin = pair_margin(scale, scalars[1], own_ids[...], mine[:rows, :], other)
        tail = jnp.exp(-jnp.abs(margin))
        weight = jnp.where(margin >= 0.0, tail, 1.0) / (1.0 + tail)
        coeff = (jnp.where(same, -scale, scale) * weight).astype(jnp.bfloat16)
        return jnp.dot(coeff, other[:rows, :], preferred_element_type=jnp.float32)

    for kind, (grad, indices) in enumerate(
        ((grad_audio, range(n_text)), (grad_text, range(n_text, count)))
    ):
        acc = term(own.at[kind], own.at[1 - kind])
        for i in indices:
            wait_load(text, held.at[i], sems, i + 2)
            acc += term(own.at[kind], held.at[i])
        grad[...] = acc.astype(jnp.bfloat16)


def call(kernel, scalars, own_ids, audio, text, texts, audios, out_shape, flops):
    blocks = tuple(texts) + tuple(audios)
    count = len(blocks)
    whole = pl.BlockSpec(memory_space=pltpu.VMEM)
    anywhere = pl.BlockSpec(memory_space=pl.ANY)
    return pl.pallas_call(
        functools.partial(kernel, len(texts), count),
        out_shape=out_shape,
        in_specs=[pl.BlockSpec(memory_space=pltpu.SMEM), whole] + [anywhere] * (2 + count),
        out_specs=jax.tree.map(lambda _: whole, out_shape),
        scratch_shapes=[
            pltpu.VMEM((2,) + text.shape, text.dtype),
            pltpu.VMEM((count,) + text.shape, text.dtype),
            pltpu.SemaphoreType.DMA((2 + count,)),
        ],
        compiler_params=pltpu.CompilerParams(vmem_limit_bytes=24 * 1024 * 1024),
        cost_estimate=pl.CostEstimate(
            flops=flops, bytes_accessed=2 * (count + 2) * text.size, transcendentals=0
        ),
    )(scalars, own_ids, audio, text, *blocks)


def losses(scalars, own_ids, audio, text, texts, audios):
    rows = own_ids.shape[0]
    return call(
        loss_kernel,
        scalars,
        own_ids,
        audio,
        text,
        texts,
        audios,
        jax.ShapeDtypeStruct((1, 128), jnp.float32),
        2 * (1 + len(texts) + len(audios)) * rows * text.size,
    )


def gradients(scalars, own_ids, audio, text, texts, audios):
    rows = own_ids.shape[0]
    shape = (rows, text.shape[1])
    return call(
        grad_kernel,
        scalars,
        own_ids,
        audio,
        text,
        texts,
        audios,
        [jax.ShapeDtypeStruct(shape, jnp.bfloat16)] * 2,
        4 * (2 + len(texts) + len(audios)) * rows * text.size,
    )


def spread_sum(row, axes):
    count = lax.axis_size(axes)
    copies = jnp.broadcast_to(row[None], (count,) + row.shape)
    return jnp.sum(lax.all_to_all(copies, axes, 0, 0, tiled=True), axis=0)


def routed(array, step):
    count = lax.axis_size(BLK)
    return lax.ppermute(array, BLK, [(i, (i + step(i)) % count) for i in range(count)])


def odd(i):
    return i % 2 == 1


def group_pairs(perm):
    forward = [(p, g) for g, p in enumerate(perm)]
    backward = [(g, p) for g, p in enumerate(perm)]
    return forward, backward, all(p == g for g, p in enumerate(perm))


def first_exchange(perm, text, audio):
    forward, _, same = group_pairs(perm)
    partner_text = text if same else lax.ppermute(text, "group", forward)
    audio2 = shifted(audio, -2)
    text4 = shifted(text, 4)
    text_x = routed(text, lambda i: 3 if odd(i) else 1)
    audio_x = core_swap(audio2)
    return (partner_text, text_x, text4), (audio2, audio_x)


def second_exchange(perm, audio, terms):
    _, backward, same = group_pairs(perm)
    partner_audio = audio if same else lax.ppermute(audio, "group", backward)
    audio4 = shifted(audio, -4)
    audio_y = routed(audio, lambda i: -1 if odd(i) else -3)
    row = spread_sum(terms, ("z",))
    return row, partner_audio, audio4, audio_y


def body(audio_embed, text_embed, caption_ids, pairing, logit_scale, logit_bias):
    rows, width = audio_embed.shape
    pair_count = rows * lax.axis_size(AXES)
    scalars = jnp.concatenate([logit_scale, logit_bias])
    high = (caption_ids // SPLIT).astype(jnp.bfloat16)
    low = (caption_ids % SPLIT).astype(jnp.bfloat16)
    marks = jnp.pad(jnp.stack([high, low]), ((0, MARKS - 2), (0, width - rows)))
    match = jnp.all(jnp.asarray(np.array(PERMS, np.int32)) == pairing[None], axis=1)
    index = jnp.sum(jnp.where(match, jnp.arange(len(PERMS), dtype=jnp.int32), 0))
    index, marks = lax.optimization_barrier((index, marks))
    text = jnp.concatenate([text_embed, marks])
    audio = jnp.concatenate([audio_embed, marks])
    own_ids = caption_ids.astype(jnp.float32).reshape(rows, 1)
    text, audio, own_ids, scalars = lax.optimization_barrier((text, audio, own_ids, scalars))
    texts, audios = lax.switch(
        index, [functools.partial(first_exchange, perm) for perm in PERMS], text, audio
    )
    terms = losses(scalars, own_ids, audio, text, texts, audios)
    text2 = shifted(after(text, texts[0]), 2)
    row, partner_audio, audio4, audio_y = lax.switch(
        index, [functools.partial(second_exchange, perm) for perm in PERMS], audio, terms
    )
    text_y = core_swap(after(text2, row))
    total = spread_sum(after(row, text_y), ("x", "yl", "core", "group"))
    grad_audio, grad_text = gradients(
        scalars,
        own_ids,
        audio,
        text,
        texts + (text2, text_y),
        audios + (audio4, audio_y, partner_audio),
    )
    return jnp.sum(total) / jnp.float32(pair_count), grad_audio, grad_text


def solution(mesh):
    inner = jax.sharding.Mesh(mesh.devices.reshape(12, 4, 2, 2, 4), AXES)
    placed = (P(AXES, None), P(AXES, None), P(AXES), P(), P(), P())
    return jax.shard_map(
        body,
        mesh=inner,
        in_specs=placed,
        out_specs=(P(), P(AXES, None), P(AXES, None)),
        check_vma=False,
    )
```
